32 devices in a mesh: comp: 2 (over core), lat: 8 (over z, y), lon: 2 (over x).
Axes of the slice: x: 2, y: 2, z: 4, core: 2. Of those that a mesh axis runs over, the one named last changes fastest.
Arguments:
- innovations: float32 [2, 3, 2048, 512], P('comp', None, ('lat', 'lon')), may hold values from -6 to 6
- obs_owner: int32 [2, 3, 2048, 1], P('comp', None, ('lat', 'lon')), may hold values from 0 to 15; in each aligned block of 128 rows (0 to 127, 128 to 255, ..., all dimensions but the last counted through in order) at most 16 rows name the same one
- obs_cell: int32 [2, 3, 2048], P('comp', None, ('lat', 'lon')), may hold values from 0 to 1023
- velocity: float32 [2, 3, 2, 128, 64, 256], P('comp', None, None, None, 'lat', 'lon'), may hold values from -0.2 to 0.2
- diffusion: float32 [2, 3, 2, 128, 64, 256], P('comp', None, None, None, 'lat', 'lon'), may hold values from 0.01 to 0.08
- mixing: float32 [2, 4, 4], P('comp'), may hold values from -0.15 to 0.15
- air_sea: float32 [4, 4], replicated, may hold values from -1 to 1
- sea_mask: int32 [64, 256], P('lat', 'lon'), may hold values 0 or 1
Outputs:
- gradient: float32 [2, 4, 128, 64, 256], P('comp', None, None, 'lat', 'lon')
The draws below stay inside these ranges and needn't reach their ends.
Inputs may be any that keep to these rules, and one draw needn't show every extreme that they name: `obs_owner`: among the 128 rows of one device for one section and timestep, no owner is named more than 16 times, a bound that some block reaches.
All inputs are finite; a program needn't handle non-finite values. No bound on the sum of `sea_mask` on one device may be relied on, other than what follows from the above.
Results may differ from the reference program's by a relative error of at most 0.0001.
Values sent between devices are 32-bit elements; how exact they have to be, the bound alone decides.
A program may use at most 320 MiB of HBM per device.

```python
import math
import jax
import jax.numpy as jnp
import numpy as np
from jax import lax

FIELDS = 4
LEV = 128
STEPS = 3
CLAT = 8
CLON = 128
OBS_DEV = 128
CAP = 16
NLAT = 64
NLON = 256
N_LAT = 8
N_LON = 2


def touch_ends(values, key, low, largest):
    extent = values.shape
    spot = [jax.random.randint(jax.random.fold_in(key, axis), (), 0, extent[axis]) for axis in range(len(extent))]
    values = values.at[tuple(spot)].set(low)
    longest = extent.index(max(extent))
    spot[longest] = (spot[longest] + 1) % extent[longest]
    return values.at[tuple(spot)].set(largest)


def block_levels(rng, shape, shards, least, largest):
    loudness = 1.0
    for dim, shards_of in shards:
        heights = jax.random.uniform(jax.random.fold_in(jax.random.fold_in(rng, 6), dim), (shards_of,), jnp.float32, least / len(shards), largest / len(shards))
        loudness = loudness * jnp.repeat(jnp.exp(heights), shape[dim] // shards_of).reshape((-1,) + (1,) * (len(shape) - 1 - dim))
    return loudness


def shared_out(stream_key, own, number, rows, count, top, most, lean):
    sequence = jax.random.permutation(stream_key, count)
    crowded, common = shares(count, rows * top, most, lean, True), shares(count, rows * top, most, lean, False)
    places = jnp.arange(count)

    def named(tallies, turn):
        used = int((tallies > 0).sum())
        fixed = max(1, used // 4)
        moved = fixed + (places - fixed + turn * (used - fixed)) % max(1, count - fixed)
        return jnp.zeros((count,), jnp.int32).at[sequence[jnp.where(places < fixed, places, moved)]].set(jnp.asarray(tallies, jnp.int32))

    tallies = jnp.where(number % 4 == 0, named(crowded, number // 4), named(common, number - number // 4 - 1))
    mixed = jax.random.permutation(jax.random.fold_in(own, 3), count)
    source_of, taker = mixed[0:count // 2 * 2:2], mixed[1:count // 2 * 2:2]
    slack = jnp.minimum(tallies[source_of] - 1, most - tallies[taker]) // 2
    slack = jnp.where((source_of == sequence[0]) | (taker == sequence[0]) | (tallies[taker] == 0), 0, jnp.maximum(slack, 0))
    moved = jax.random.randint(jax.random.fold_in(own, 4), (count // 2,), 0, 1 << 20) % (slack + 1)
    tallies = tallies.at[source_of].add(-moved).at[taker].add(moved)
    members = jnp.searchsorted(jnp.cumsum(tallies), jnp.arange(rows * top), side="right").astype(jnp.int32)
    listing = members.reshape(top, rows).T
    listing = listing[jax.random.permutation(jax.random.fold_in(own, 1), rows)]
    turn = jax.random.randint(jax.random.fold_in(own, 2), (rows, 1), 0, top)
    return jnp.take_along_axis(listing, (jnp.arange(top)[None, :] + turn) % top, axis=1)


def shares(count, total, limit, lean, full):
    weights = [(1 << 20) // math.isqrt(grade ** lean) + 1 for grade in range(1, count + 1)]
    largest = limit if full else min(limit, max(-(-total // count), total * weights[0] // sum(weights)))
    least = 1 if total - largest >= count - 1 else 0
    holding, rest = [largest] + [least] * (count - 1), total - largest - least * (count - 1)
    while rest > 0:
        candidates = [i for i in range(1, count) if holding[i] < largest] or [i for i in range(1, count) if holding[i] < limit]
        mass, left = sum([weights[i] for i in candidates]), rest
        for i in candidates:
            more = min(limit - holding[i], max(1, left * weights[i] // mass), rest)
            holding[i] = holding[i] + more
            rest = rest - more
    return np.array(holding)


def bell_draw(own_key, extent, deviation, limit, shards=(), kind=jnp.bfloat16):
    gain = block_levels(own_key, extent, shards, -0.22, 0.18) if shards else 1.0
    drawn = jax.random.normal(own_key, extent, jnp.float32) * deviation * gain
    return jnp.minimum(jnp.maximum(drawn, -limit), limit).astype(kind)


def setup_inputs(seed: int = 0) -> dict:
    keys = jax.random.split(jax.random.key(seed), 9)
    innovations = bell_draw(keys[0], (2, STEPS, N_LAT * N_LON * OBS_DEV, FIELDS * LEV), 1.0, 6.0, ((0, 2), (2, 16)), jnp.float32)
    obs_owner_keys = jax.random.split(jax.random.fold_in(keys[1], 1), 2 * STEPS * (N_LAT * N_LON * OBS_DEV) // OBS_DEV)
    obs_owner_turns = jax.random.permutation(jax.random.fold_in(keys[1], 3), 2 * STEPS * (N_LAT * N_LON * OBS_DEV) // OBS_DEV)
    obs_owner = jax.vmap(lambda own, number: shared_out(jax.random.fold_in(keys[1], 2), own, number, OBS_DEV, N_LAT * N_LON, 1, CAP, 2))(obs_owner_keys, obs_owner_turns).reshape((2, STEPS, N_LAT * N_LON * OBS_DEV, 1))
    obs_cell = touch_ends(jax.random.randint(keys[2], (2, STEPS, N_LAT * N_LON * OBS_DEV), 0, CLAT * CLON), jax.random.fold_in(keys[2], 1), 0, (CLAT * CLON) - 1).astype(jnp.int32)
    velocity = jnp.clip(jax.random.uniform(keys[3], (2, STEPS, 2, LEV, NLAT, NLON), jnp.float32, -0.2, 0.2) * block_levels(keys[3], (2, STEPS, 2, LEV, NLAT, NLON), ((0, 2), (4, 8), (5, 2)), -0.4, 0.0), -0.2, 0.2)
    diffusion = jnp.clip(jnp.exp(math.log(0.08) - 2.0794415 * jax.random.uniform(keys[4], (2, STEPS, 2, LEV, NLAT, NLON), jnp.float32) ** block_levels(keys[4], (2, STEPS, 2, LEV, NLAT, NLON), ((0, 2), (4, 8), (5, 2)), -0.2, 0.2)), 0.01, 0.08)
    mixing = jnp.clip(jax.random.uniform(keys[5], (2, FIELDS, FIELDS), jnp.float32, -0.15, 0.15) * block_levels(keys[5], (2, FIELDS, FIELDS), ((0, 2),), -0.4, 0.0), -0.15, 0.15)
    air_sea = jnp.clip(jax.random.uniform(keys[6], (FIELDS, FIELDS), jnp.float32, -1.0, 1.0), -1.0, 1.0)
    sea_mask = touch_ends((jax.random.randint(keys[7], (NLAT, NLON), 0, 3) < 2).astype(jnp.int32), jax.random.fold_in(keys[7], 1), 0, 1)
    return dict(innovations=innovations, obs_owner=obs_owner, obs_cell=obs_cell, velocity=velocity, diffusion=diffusion, mixing=mixing, air_sea=air_sea, sea_mask=sea_mask)


HIGH = lax.Precision.HIGHEST


def place_rows(rows, owner, cell):
    lat_block = owner // N_LON
    lon_block = owner % N_LON
    row_index = lat_block * CLAT + cell // CLON
    col_index = lon_block * CLON + cell % CLON
    flat_index = (row_index * NLON + col_index).astype(jnp.int32)
    total = jnp.zeros((NLAT * NLON, FIELDS * LEV), jnp.float32).at[flat_index].add(rows)
    return jnp.transpose(total.reshape(NLAT, NLON, FIELDS, LEV), (2, 3, 0, 1))


def adjoint_step(adjoint, speeds, diffuse, mixing, air_sea, sea_float):
    masked = jnp.stack([adjoint[0], adjoint[1] * sea_float])
    result = masked + jnp.einsum("sfg,sflyx->sglyx", mixing, masked, precision=HIGH)
    east_up = (jnp.maximum(speeds[:, 0], 0.0) + diffuse[:, 0])[:, None]
    east_down = (jnp.minimum(speeds[:, 0], 0.0) - diffuse[:, 0])[:, None]
    east_diff = jnp.roll(masked, -1, axis=4) - masked
    result = result + east_up * east_diff + jnp.roll(east_down * east_diff, 1, axis=4)
    open_rows = (jnp.arange(NLAT) < NLAT - 1).astype(jnp.float32)[:, None]
    north_up = ((jnp.maximum(speeds[:, 1], 0.0) + diffuse[:, 1]) * open_rows)[:, None]
    north_down = ((jnp.minimum(speeds[:, 1], 0.0) - diffuse[:, 1]) * open_rows)[:, None]
    north_next = jnp.concatenate([masked[:, :, :, 1:], jnp.zeros_like(masked[:, :, :, :1])], axis=3)
    north_diff = north_next - masked
    carried = north_down * north_diff
    shifted = jnp.concatenate([jnp.zeros_like(carried[:, :, :, :1]), carried[:, :, :, :-1]], axis=3)
    result = result + north_up * north_diff + shifted
    coupled = sea_float * jnp.einsum("fg,fyx->gyx", air_sea, masked[0, :, LEV - 1], precision=HIGH)
    return result.at[1, :, 0].add(coupled)


def reference(innovations, obs_owner, obs_cell, velocity, diffusion, mixing, air_sea, sea_mask):
    sea_float = sea_mask.astype(jnp.float32)
    adjoint = jnp.zeros((2, FIELDS, LEV, NLAT, NLON), jnp.float32)
    for step in reversed(range(STEPS)):
        forcing = jnp.stack([place_rows(innovations[section, step], obs_owner[section, step, :, 0], obs_cell[section, step]) for section in range(2)])
        adjoint = adjoint + forcing
        adjoint = adjoint_step(adjoint, velocity[:, step], diffusion[:, step], mixing, air_sea, sea_float)
    return adjoint
```

```python
import functools

import jax
import jax.numpy as jnp
from jax import lax
from jax.experimental import pallas as pl
from jax.experimental.pallas import tpu as pltpu
from jax.sharding import PartitionSpec as P

MESH = pl.DeviceIdType.MESH
LANES = 128
SUB = 8


def split3(x):
    hi = x.astype(jnp.bfloat16)
    rest = x - hi.astype(jnp.float32)
    mid = rest.astype(jnp.bfloat16)
    lo = (rest - mid.astype(jnp.float32)).astype(jnp.bfloat16)
    return hi, mid, lo


def sweep(
    dims,
    innov,
    owner_ref,
    cell_ref,
    vel,
    dif,
    mix_ref,
    air_ref,
    sea_ref,
    out_ref,
    inn_v,
    vel_v,
    dif_v,
    send,
    recv,
    cells_s,
    cells_r,
    rimn_s,
    rimn_r,
    rime_s,
    rime_r,
    state,
    halo,
    side_s,
    side_r,
    top_s,
    top_r,
    spread,
    place,
    load_sem,
    data_ss,
    data_rs,
    cell_ss,
    cell_rs,
    rim_ss,
    rim_rs,
    halo_ss,
    halo_rs,
    side_ss,
    side_rs,
    top_ss,
    top_rs,
):
    steps, fields, levels, rows, obs, lat_n, lon_n, cap = dims
    n = lat_n * lon_n
    slots = n * cap
    tiles = slots // LANES
    per_tile = LANES // cap
    fl = fields * levels
    blocks = levels // SUB
    comp = lax.axis_index("comp")
    lat = lax.axis_index("lat")
    lon = lax.axis_index("lon")
    me = lat * lon_n + lon
    east = lax.rem(lon + 1, lon_n)
    west = lax.rem(lon + lon_n - 1, lon_n)
    is_ocean = comp == 1
    order = list(reversed(range(steps)))

    def at_offset(k):
        peer = lax.rem(me + k, n)
        return (comp, peer // lon_n, lax.rem(peer, lon_n))

    loads = {}
    for t in order:
        loads["i", t] = pltpu.make_async_copy(innov.at[t], inn_v.at[t], load_sem.at[0, t])
        loads["i", t].start()
    for t in order:
        loads["v", t] = pltpu.make_async_copy(vel.at[t], vel_v.at[t], load_sem.at[1, t])
        loads["d", t] = pltpu.make_async_copy(dif.at[t], dif_v.at[t], load_sem.at[2, t])
        loads["v", t].start()
        loads["d", t].start()

    barrier = pltpu.get_barrier_semaphore()

    @pl.loop(1, n)
    def _(k):
        pl.semaphore_signal(barrier, inc=1, device_id=at_offset(k), device_id_type=MESH)

    pl.semaphore_signal(barrier, inc=1, device_id=(1 - comp, lat, lon), device_id_type=MESH)

    sub_i = lax.broadcasted_iota(jnp.int32, (obs, obs), 0)
    lane_i = lax.broadcasted_iota(jnp.int32, (obs, obs), 1)
    earlier = sub_i < lane_i
    lane1 = lax.broadcasted_iota(jnp.int32, (1, LANES), 1)
    lane8 = lax.broadcasted_iota(jnp.int32, (SUB, LANES), 1)

    def picks(t):
        owner = owner_ref[t : t + 1, :]
        across = jnp.broadcast_to(owner.astype(jnp.float32), (obs, obs))
        down = across.T
        rank = jnp.sum(
            jnp.where((across == down) & earlier, 1.0, 0.0), axis=0, keepdims=True
        ).astype(jnp.int32)
        shift = owner - me
        offset = jnp.where(shift < 0, shift + n, shift)
        target = offset * cap + rank
        slot_i = lax.broadcasted_iota(jnp.int32, (slots, obs), 0)
        return jnp.where(slot_i == target, 1.0, 0.0)

    for t in order:
        hot = picks(t)
        cells = jnp.broadcast_to(cell_ref[t : t + 1, :].astype(jnp.float32) + 1.0, (SUB, obs))
        at = (
            lax.dot_general(
                cells,
                hot,
                (((1,), (1,)), ((), ())),
                precision=lax.Precision.HIGHEST,
                preferred_element_type=jnp.float32,
            )
            - 1.0
        )
        for i in range(tiles):
            cells_s[i, t : t + 1, :] = at[0:1, i * LANES : (i + 1) * LANES]

    pl.semaphore_wait(barrier, n)

    def cell_copy(k):
        return pltpu.make_async_remote_copy(
            src_ref=cells_s.at[k // per_tile],
            dst_ref=cells_r.at[k],
            send_sem=cell_ss.at[k],
            recv_sem=cell_rs.at[k],
            device_id=at_offset(k),
            device_id_type=MESH,
        )

    def data_copy(t, k):
        return pltpu.make_async_remote_copy(
            src_ref=send.at[t, k],
            dst_ref=recv.at[t, k],
            send_sem=data_ss.at[t, k],
            recv_sem=data_rs.at[t, k],
            device_id=at_offset(k),
            device_id_type=MESH,
        )

    def north_rim_copy():
        return pltpu.make_async_remote_copy(
            src_ref=rimn_s,
            dst_ref=rimn_r,
            send_sem=rim_ss.at[0],
            recv_sem=rim_rs.at[0],
            device_id=(comp, lax.rem(lat + 1, lat_n), lon),
            device_id_type=MESH,
        )

    def east_rim_copy():
        return pltpu.make_async_remote_copy(
            src_ref=rime_s,
            dst_ref=rime_r,
            send_sem=rim_ss.at[1],
            recv_sem=rim_rs.at[1],
            device_id=(comp, lat, east),
            device_id_type=MESH,
        )

    def halo_copy(t, up):
        return pltpu.make_async_remote_copy(
            src_ref=state.at[t, rows - 1 if up else 0],
            dst_ref=halo.at[t, 0 if up else 1],
            send_sem=halo_ss.at[t, 0 if up else 1],
            recv_sem=halo_rs.at[t, 0 if up else 1],
            device_id=(comp, lax.rem(lat + (1 if up else lat_n - 1), lat_n), lon),
            device_id_type=MESH,
        )

    def side_copy(t, to_east):
        return pltpu.make_async_remote_copy(
            src_ref=side_s.at[t],
            dst_ref=side_r.at[t, 1 if to_east else 0],
            send_sem=side_ss.at[t, 1 if to_east else 0],
            recv_sem=side_rs.at[t, 1 if to_east else 0],
            device_id=(comp, lat, east if to_east else west),
            device_id_type=MESH,
        )

    def top_copy(t):
        return pltpu.make_async_remote_copy(
            src_ref=top_s.at[t],
            dst_ref=top_r.at[t],
            send_sem=top_ss.at[t],
            recv_sem=top_rs.at[t],
            device_id=(1 - comp, lat, lon),
            device_id_type=MESH,
        )

    sides = (True,) if lon_n == 2 else (True, False)
    not_last = lat < lat_n - 1
    not_first = lat > 0

    @pl.loop(1, n)
    def _(k):
        cell_copy(k).start()

    for i in range(1):
        cells_r[0] = cells_s[0]

    def pack(t):
        loads["i", t].wait()
        hot = picks(t).astype(jnp.bfloat16)
        hi, mid, lo = split3(inn_v[t])
        packed = jnp.dot(
            jnp.concatenate([hot, hot, hot], axis=1),
            jnp.concatenate([hi, mid, lo], axis=0),
            preferred_element_type=jnp.float32,
        ).reshape(n, cap, fl)
        send[t] = packed
        recv[t, 0] = packed[0]

    def ship(t):
        @pl.loop(1, n)
        def _(k):
            data_copy(t, k).start()

    pack(order[0])
    ship(order[0])

    for t in order:
        loads["v", t].wait()
        loads["d", t].wait()

        @pl.loop(0, blocks)
        def _(b):
            edge = pl.ds(b * (SUB * rows) + rows - 1, SUB, stride=rows)
            fall = jnp.minimum(vel_v[t, 1, edge, :], 0.0) - dif_v[t, 1, edge, :]
            rimn_s[t, pl.ds(pl.multiple_of(b * SUB, SUB), SUB), :] = fall
            packed = rime_s[t]
            for y in range(rows):
                line = pl.ds(b * (SUB * rows) + y, SUB, stride=rows)
                fall = jnp.minimum(vel_v[t, 0, line, :], 0.0) - dif_v[t, 0, line, :]
                q = b * rows + y
                packed = jnp.where(lane8 == q, pltpu.roll(fall, lax.rem(q + 1, LANES), 1), packed)
            rime_s[t] = packed

    @pl.when(not_last)
    def _():
        north_rim_copy().start()

    east_rim_copy().start()

    @pl.when(jnp.logical_not(not_first))
    def _():
        rimn_r[...] = jnp.zeros_like(rimn_r)
        for t in order:
            halo[t, 0] = jnp.zeros((fl, LANES), jnp.float32)

    @pl.when(jnp.logical_not(not_last))
    def _():
        for t in order:
            halo[t, 1] = jnp.zeros((fl, LANES), jnp.float32)

    for t in order[1:]:
        pack(t)
    if steps > 1:
        ship(order[1])

    @pl.loop(1, n)
    def _(k):
        cell_copy(k).wait_recv()

    land = [
        jnp.where(is_ocean, sea_ref[y : y + 1, :].astype(jnp.float32), 1.0) for y in range(rows)
    ]
    open_last = jnp.where(not_last, 1.0, 0.0)

    for turn, t in enumerate(order):
        first = turn == 0

        @pl.loop(1, n)
        def _(k):
            data_copy(t, k).wait_recv()

        for i in range(tiles):
            line = jnp.full((1, LANES), -1.0, jnp.float32)
            for j in range(per_tile):
                k = i * per_tile + j
                line = jnp.where(lane1 // cap == j, cells_r[k, t : t + 1, :], line)
            place[i * LANES : (i + 1) * LANES, :] = jnp.broadcast_to(line, (LANES, LANES)).T

        for i in range(tiles):
            part = recv[t, i * per_tile : (i + 1) * per_tile].reshape(LANES, fl)
            hi, mid, lo = split3(part.T)
            spread[:, i * LANES : (i + 1) * LANES] = hi
            spread[:, slots + i * LANES : slots + (i + 1) * LANES] = mid
            spread[:, 2 * slots + i * LANES : 2 * slots + (i + 1) * LANES] = lo

        def add_forcing(y):
            lane_s = lax.broadcasted_iota(jnp.int32, (slots, LANES), 1)
            col = lane_s.astype(jnp.float32)
            where_to = place[...]
            hot = jnp.concatenate(
                [
                    jnp.where(where_to == col + float(v * LANES), 1.0, 0.0).astype(jnp.bfloat16)
                    for v in (y, y + 1)
                ],
                axis=1,
            )
            hot3 = jnp.concatenate([hot, hot, hot], axis=0)
            for f in range(fields):
                part = slice(f * levels, (f + 1) * levels)
                got = jnp.dot(spread[part, :], hot3, preferred_element_type=jnp.float32)
                for v in (0, 1):
                    new = got[:, v * LANES : (v + 1) * LANES]
                    if not first:
                        new = new + state[t, y + v, part, :]
                    state[t, y + v, part, :] = new * land[y + v]

        add_forcing(0)

        @pl.when(not_first)
        def _():
            halo_copy(t, False).start()

        add_forcing(rows - 2)

        @pl.when(not_last)
        def _():
            halo_copy(t, True).start()

        for y in range(2, rows - 2, 2):
            add_forcing(y)

        @pl.loop(0, blocks)
        def _(b):
            half = b // SUB
            dst = pl.ds(pl.multiple_of(lax.rem(b, SUB) * SUB, SUB), SUB)
            packed = side_s[t, dst, :]
            for y in range(rows):
                for f in range(fields):
                    q = half * (rows * fields) + y * fields + f
                    src = pl.ds(pl.multiple_of(f * levels + b * SUB, SUB), SUB)
                    turned = pltpu.roll(state[t, y, src, :], 2 * q + 1, 1)
                    packed = jnp.where(lane8 // 2 == q, turned, packed)
            side_s[t, dst, :] = packed

        for to_east in sides:
            side_copy(t, to_east).start()

        @pl.when(jnp.logical_not(is_ocean))
        def _():
            for f in range(fields):
                for y in range(rows):
                    at = f * levels + levels - 1
                    top_s[t, f * rows + y : f * rows + y + 1, :] = state[t, y, at : at + 1, :]
            top_copy(t).start()

        if turn + 2 < steps:
            ship(order[turn + 2])

        if first:

            @pl.when(not_first)
            def _():
                north_rim_copy().wait_recv()

            east_rim_copy().wait_recv()

        for to_east in sides:
            side_copy(t, to_east).wait_recv()

        @pl.when(not_first)
        def _():
            halo_copy(t, True).wait_recv()

        @pl.when(not_last)
        def _():
            halo_copy(t, False).wait_recv()

        last = turn == steps - 1

        @pl.loop(0, blocks)
        def _(b):
            half = b // SUB
            lev = pl.ds(pl.multiple_of(b * SUB, SUB), SUB)
            fls = [pl.ds(pl.multiple_of(f * levels + b * SUB, SUB), SUB) for f in range(fields)]
            lo = pl.ds(pl.multiple_of(lax.rem(b, SUB) * SUB, SUB), SUB)
            if lon_n == 2:
                edge = side_r[t, 1, lo, :]
            else:
                edge = jnp.where(lax.rem(lane8, 2) == 1, side_r[t, 0, lo, :], side_r[t, 1, lo, :])
            rim_e = rime_r[t]
            below = [halo[t, 0, s, :] for s in fls]
            here = [state[t, 0, s, :] for s in fls]
            fall_n = rimn_r[t, lev, :]
            for y in range(rows):
                if y < rows - 1:
                    above = [state[t, y + 1, s, :] for s in fls]
                else:
                    above = [halo[t, 1, s, :] for s in fls]
                line = pl.ds(b * (SUB * rows) + y, SUB, stride=rows)
                we, ke = vel_v[t, 0, line, :], dif_v[t, 0, line, :]
                wn, kn = vel_v[t, 1, line, :], dif_v[t, 1, line, :]
                up_e = jnp.maximum(we, 0.0) + ke
                fall_e = pltpu.roll(jnp.minimum(we, 0.0) - ke, 1, 1)
                from_west = pltpu.roll(rim_e, lax.rem(LANES - (b * rows + y), LANES), 1)
                fall_e = jnp.where(lane8 == 0, from_west, fall_e)
                up_n = jnp.maximum(wn, 0.0) + kn
                next_fall = jnp.minimum(wn, 0.0) - kn
                if y == rows - 1:
                    up_n = up_n * open_last
                for g in range(fields):
                    m = here[g]
                    q = half * (rows * fields) + y * fields + g
                    rim = pltpu.roll(edge, LANES - 1 - 2 * q, 1)
                    m_east = pltpu.roll(jnp.where(lane8 == 0, rim, m), LANES - 1, 1)
                    m_west = pltpu.roll(jnp.where(lane8 == LANES - 1, rim, m), 1, 1)
                    res = m
                    for f in range(fields):
                        res = res + mix_ref[f, g] * here[f]
                    res = res + up_e * (m_east - m) + fall_e * (m - m_west)
                    res = res + up_n * (above[g] - m) + fall_n * (m - below[g])
                    if last:
                        spot = pl.ds(
                            g * (levels * rows) + b * (SUB * rows) + y, SUB, stride=rows
                        )
                        out_ref[spot, :] = res
                    else:
                        state[order[turn + 1] if not last else 0, y, fls[g], :] = res
                below, here, fall_n = here, above, next_fall

        @pl.when(is_ocean)
        def _():
            top_copy(t).wait_recv()
            for g in range(fields):
                flux = air_ref[0, g] * top_r[t, 0:rows, :]
                for f in range(1, fields):
                    flux = flux + air_ref[f, g] * top_r[t, f * rows : (f + 1) * rows, :]
                flux = flux * sea_ref[...].astype(jnp.float32)
                if last:
                    spot = slice(g * levels * rows, g * levels * rows + rows)
                    out_ref[spot, :] = out_ref[spot, :] + flux
                else:
                    nxt = order[turn + 1]
                    at = g * levels
                    for y in range(rows):
                        state[nxt, y, at : at + 1, :] = (
                            state[nxt, y, at : at + 1, :] + flux[y : y + 1, :]
                        )

    @pl.loop(1, n)
    def _(k):
        cell_copy(k).wait_send()
        for t in order:
            data_copy(t, k).wait_send()

    east_rim_copy().wait_send()

    @pl.when(not_last)
    def _():
        north_rim_copy().wait_send()

    for t in order:
        for to_east in sides:
            side_copy(t, to_east).wait_send()

        @pl.when(not_first)
        def _():
            halo_copy(t, False).wait_send()

        @pl.when(not_last)
        def _():
            halo_copy(t, True).wait_send()

        @pl.when(jnp.logical_not(is_ocean))
        def _():
            top_copy(t).wait_send()


def shards(lat_n, lon_n, innovations, obs_owner, obs_cell, velocity, diffusion, mixing, air_sea, sea_mask):
    steps, levels, rows, cols = (velocity.shape[i] for i in (1, 3, 4, 5))
    fields = mixing.shape[1]
    obs = innovations.shape[2]
    fl = fields * levels
    n = lat_n * lon_n
    cap = max(SUB, 2 * obs // n)
    slots = n * cap
    tiles = slots // LANES
    dims = (steps, fields, levels, rows, obs, lat_n, lon_n, cap)
    vmem = pl.BlockSpec(memory_space=pltpu.VMEM)
    smem = pl.BlockSpec(memory_space=pltpu.SMEM)
    hbm = pl.BlockSpec(memory_space=pl.ANY)
    f32 = jnp.float32
    dma = pltpu.SemaphoreType.DMA
    out = pl.pallas_call(
        functools.partial(sweep, dims),
        out_shape=jax.ShapeDtypeStruct((fl * rows, cols), f32),
        in_specs=[hbm, vmem, vmem, hbm, hbm, smem, smem, vmem],
        out_specs=vmem,
        scratch_shapes=[
            pltpu.VMEM((steps, obs, fl), f32),
            pltpu.VMEM((steps, 2, levels * rows, cols), f32),
            pltpu.VMEM((steps, 2, levels * rows, cols), f32),
            pltpu.VMEM((steps, n, cap, fl), f32),
            pltpu.VMEM((steps, n, cap, fl), f32),
            pltpu.VMEM((tiles, SUB, LANES), f32),
            pltpu.VMEM((n, SUB, LANES), f32),
            pltpu.VMEM((steps, levels, cols), f32),
            pltpu.VMEM((steps, levels, cols), f32),
            pltpu.VMEM((steps, SUB, cols), f32),
            pltpu.VMEM((steps, SUB, cols), f32),
            pltpu.VMEM((steps, rows, fl, cols), f32),
            pltpu.VMEM((steps, 2, fl, cols), f32),
            pltpu.VMEM((steps, SUB * SUB, cols), f32),
            pltpu.VMEM((steps, 2, SUB * SUB, cols), f32),
            pltpu.VMEM((steps, fields * rows, cols), f32),
            pltpu.VMEM((steps, fields * rows, cols), f32),
            pltpu.VMEM((fl, 3 * slots), jnp.bfloat16),
            pltpu.VMEM((slots, LANES), f32),
            dma((3, steps)),
            dma((steps, n)),
            dma((steps, n)),
            dma((n,)),
            dma((n,)),
            dma((2,)),
            dma((2,)),
            dma((steps, 2)),
            dma((steps, 2)),
            dma((steps, 2)),
            dma((steps, 2)),
            dma((steps,)),
            dma((steps,)),
        ],
        compiler_params=pltpu.CompilerParams(
            collective_id=0, has_side_effects=True, vmem_limit_bytes=56 * 1024 * 1024
        ),
    )(
        innovations[0],
        obs_owner[0, :, :, 0],
        obs_cell[0],
        velocity[0].reshape(steps, 2, levels * rows, cols),
        diffusion[0].reshape(steps, 2, levels * rows, cols),
        mixing[0],
        air_sea,
        sea_mask,
    )
    return out.reshape(1, fields, levels, rows, cols)


def solution(mesh):
    return jax.shard_map(
        functools.partial(shards, mesh.shape["lat"], mesh.shape["lon"]),
        mesh=mesh,
        in_specs=(
            P("comp", None, ("lat", "lon"), None),
            P("comp", None, ("lat", "lon"), None),
            P("comp", None, ("lat", "lon")),
            P("comp", None, None, None, "lat", "lon"),
            P("comp", None, None, None, "lat", "lon"),
            P("comp", None, None),
            P(),
            P("lat", "lon"),
        ),
        out_specs=P("comp", None, None, "lat", "lon"),
        check_vma=False,
    )
```

```python
import functools

import jax
import jax.numpy as jnp
from jax import lax
from jax.experimental import pallas as pl
from jax.experimental.pallas import tpu as pltpu
from jax.sharding import PartitionSpec as P

MESH = pl.DeviceIdType.MESH
LANES = 128
SUB = 8


def split3(x):
    hi = x.astype(jnp.bfloat16)
    rest = x - hi.astype(jnp.float32)
    mid = rest.astype(jnp.bfloat16)
    lo = (rest - mid.astype(jnp.float32)).astype(jnp.bfloat16)
    return hi, mid, lo


def sweep(
    dims,
    innov,
    owner_ref,
    cell_ref,
    vel,
    dif,
    mix_ref,
    air_ref,
    sea_ref,
    out_ref,
    inn_v,
    vel_v,
    dif_v,
    send,
    recv,
    cells_s,
    cells_r,
    rimn_s,
    rimn_r,
    rime_s,
    rime_r,
    state,
    halo,
    side_s,
    side_r,
    top_s,
    top_r,
    spread,
    place,
    load_sem,
    data_ss,
    data_rs,
    cell_ss,
    cell_rs,
    rim_ss,
    rim_rs,
    halo_ss,
    halo_rs,
    side_ss,
    side_rs,
    top_ss,
    top_rs,
):
    steps, fields, levels, rows, obs, lat_n, lon_n, cap, chunks, lag, window = dims
    n = lat_n * lon_n
    slots = n * cap
    tiles = slots // LANES
    per_tile = LANES // cap
    fl = fields * levels
    blocks = levels // SUB
    depth = levels // chunks
    width = fields * depth
    chunk_blocks = depth // SUB
    comp = lax.axis_index("comp")
    lat = lax.axis_index("lat")
    lon = lax.axis_index("lon")
    me = lat * lon_n + lon
    east = lax.rem(lon + 1, lon_n)
    west = lax.rem(lon + lon_n - 1, lon_n)
    is_ocean = comp == 1
    order = list(reversed(range(steps)))
    units = [(t, c) for t in order for c in range(chunks)]

    def at_offset(k):
        peer = lax.rem(me + k, n)
        return (comp, peer // lon_n, lax.rem(peer, lon_n))

    loads = {}
    for t in order:
        loads["i", t] = pltpu.make_async_copy(innov.at[t], inn_v.at[t], load_sem.at[0, t])
        loads["i", t].start()
    for t in order:
        loads["v", t] = pltpu.make_async_copy(vel.at[t], vel_v.at[t], load_sem.at[1, t])
        loads["d", t] = pltpu.make_async_copy(dif.at[t], dif_v.at[t], load_sem.at[2, t])
        loads["v", t].start()
        loads["d", t].start()

    barrier = pltpu.get_barrier_semaphore()

    @pl.loop(1, n)
    def _(k):
        pl.semaphore_signal(barrier, inc=1, device_id=at_offset(k), device_id_type=MESH)

    pl.semaphore_signal(barrier, inc=1, device_id=(1 - comp, lat, lon), device_id_type=MESH)

    sub_i = lax.broadcasted_iota(jnp.int32, (obs, obs), 0)
    lane_i = lax.broadcasted_iota(jnp.int32, (obs, obs), 1)
    earlier = sub_i < lane_i
    lane1 = lax.broadcasted_iota(jnp.int32, (1, LANES), 1)
    lane8 = lax.broadcasted_iota(jnp.int32, (SUB, LANES), 1)

    def picks(t):
        owner = owner_ref[t]
        across = jnp.broadcast_to(owner.astype(jnp.float32), (obs, obs))
        down = across.T
        rank = jnp.sum(
            jnp.where((across == down) & earlier, 1.0, 0.0), axis=0, keepdims=True
        ).astype(jnp.int32)
        shift = owner - me
        offset = jnp.where(shift < 0, shift + n, shift)
        target = offset * cap + rank
        slot_i = lax.broadcasted_iota(jnp.int32, (slots, obs), 0)
        return jnp.where(slot_i == target, 1.0, 0.0)

    for t in order:
        hot = picks(t)
        cells = jnp.broadcast_to(cell_ref[t].astype(jnp.float32) + 1.0, (SUB, obs))
        at = (
            lax.dot_general(
                cells,
                hot,
                (((1,), (1,)), ((), ())),
                precision=lax.Precision.HIGHEST,
                preferred_element_type=jnp.float32,
            )
            - 1.0
        )
        for i in range(tiles):
            cells_s[i, t : t + 1, :] = at[0:1, i * LANES : (i + 1) * LANES]

    pl.semaphore_wait(barrier, n)

    def cell_copy(k):
        return pltpu.make_async_remote_copy(
            src_ref=cells_s.at[k // per_tile],
            dst_ref=cells_r.at[k],
            send_sem=cell_ss.at[k],
            recv_sem=cell_rs.at[k],
            device_id=at_offset(k),
            device_id_type=MESH,
        )

    def data_copy(t, c, k):
        return pltpu.make_async_remote_copy(
            src_ref=send.at[t, c, k],
            dst_ref=recv.at[t, c, k],
            send_sem=data_ss.at[t * chunks + c, k],
            recv_sem=data_rs.at[t * chunks + c, k],
            device_id=at_offset(k),
            device_id_type=MESH,
        )

    def north_rim_copy():
        return pltpu.make_async_remote_copy(
            src_ref=rimn_s,
            dst_ref=rimn_r,
            send_sem=rim_ss.at[0],
            recv_sem=rim_rs.at[0],
            device_id=(comp, lax.rem(lat + 1, lat_n), lon),
            device_id_type=MESH,
        )

    def east_rim_copy():
        return pltpu.make_async_remote_copy(
            src_ref=rime_s,
            dst_ref=rime_r,
            send_sem=rim_ss.at[1],
            recv_sem=rim_rs.at[1],
            device_id=(comp, lat, east),
            device_id_type=MESH,
        )

    def halo_copy(t, c, up):
        part = pl.ds(c * width, width)
        return pltpu.make_async_remote_copy(
            src_ref=state.at[t, rows - 1 if up else 0, part],
            dst_ref=halo.at[t, 0 if up else 1, part],
            send_sem=halo_ss.at[t * chunks + c, 0 if up else 1],
            recv_sem=halo_rs.at[t * chunks + c, 0 if up else 1],
            device_id=(comp, lax.rem(lat + (1 if up else lat_n - 1), lat_n), lon),
            device_id_type=MESH,
        )

    def side_copy(t, c, to_east):
        return pltpu.make_async_remote_copy(
            src_ref=side_s.at[t, c],
            dst_ref=side_r.at[t, c, 1 if to_east else 0],
            send_sem=side_ss.at[t * chunks + c, 1 if to_east else 0],
            recv_sem=side_rs.at[t * chunks + c, 1 if to_east else 0],
            device_id=(comp, lat, east if to_east else west),
            device_id_type=MESH,
        )

    def top_copy(t):
        return pltpu.make_async_remote_copy(
            src_ref=top_s.at[t],
            dst_ref=top_r.at[t],
            send_sem=top_ss.at[t],
            recv_sem=top_rs.at[t],
            device_id=(1 - comp, lat, lon),
            device_id_type=MESH,
        )

    sides = (True,) if lon_n == 2 else (True, False)
    not_last = lat < lat_n - 1
    not_first = lat > 0

    @pl.loop(1, n)
    def _(k):
        cell_copy(k).start()

    cells_r[0] = cells_s[0]

    def pack(t):
        loads["i", t].wait()
        hot = picks(t).astype(jnp.bfloat16)
        wide = inn_v[t]
        by_chunk = jnp.concatenate(
            [
                wide[:, f * levels + c * depth : f * levels + (c + 1) * depth]
                for c in range(chunks)
                for f in range(fields)
            ],
            axis=1,
        )
        hi, mid, lo = split3(by_chunk)
        packed = jnp.dot(
            jnp.concatenate([hot, hot, hot], axis=1),
            jnp.concatenate([hi, mid, lo], axis=0),
            preferred_element_type=jnp.float32,
        )
        for c in range(chunks):
            part = packed[:, c * width : (c + 1) * width].reshape(n, cap, width)
            send[t, c] = part
            recv[t, c, 0] = part[0]

    def ship(t, c):
        @pl.loop(1, n)
        def _(k):
            data_copy(t, c, k).start()

    packed_to = 1
    pack(order[0])
    for i in range(min(window, len(units))):
        while order.index(units[i][0]) >= packed_to:
            pack(order[packed_to])
            packed_to += 1
        ship(*units[i])

    for t in order:
        loads["v", t].wait()
        loads["d", t].wait()

        @pl.loop(0, blocks)
        def _(b):
            edge = pl.ds(b * (SUB * rows) + rows - 1, SUB, stride=rows)
            fall = jnp.minimum(vel_v[t, 1, edge, :], 0.0) - dif_v[t, 1, edge, :]
            rimn_s[t, pl.ds(pl.multiple_of(b * SUB, SUB), SUB), :] = fall
            packed = rime_s[t]
            for y in range(rows):
                line = pl.ds(b * (SUB * rows) + y, SUB, stride=rows)
                fall = jnp.minimum(vel_v[t, 0, line, :], 0.0) - dif_v[t, 0, line, :]
                q = b * rows + y
                packed = jnp.where(lane8 == q, pltpu.roll(fall, lax.rem(q + 1, LANES), 1), packed)
            rime_s[t] = packed

    @pl.when(not_last)
    def _():
        north_rim_copy().start()

    east_rim_copy().start()

    @pl.when(jnp.logical_not(not_first))
    def _():
        rimn_r[...] = jnp.zeros_like(rimn_r)
        for t in order:
            halo[t, 0] = jnp.zeros((fl, LANES), jnp.float32)

    @pl.when(jnp.logical_not(not_last))
    def _():
        for t in order:
            halo[t, 1] = jnp.zeros((fl, LANES), jnp.float32)

    for t in order[packed_to:]:
        pack(t)

    @pl.loop(1, n)
    def _(k):
        cell_copy(k).wait_recv()

    land = [
        jnp.where(is_ocean, sea_ref[y : y + 1, :].astype(jnp.float32), 1.0) for y in range(rows)
    ]
    open_last = jnp.where(not_last, 1.0, 0.0)

    def forced_unit(i):
        t, c = units[i]
        first = t == order[0]
        base = c * width

        @pl.loop(1, n)
        def _(k):
            data_copy(t, c, k).wait_recv()

        if i + window < len(units):
            ship(*units[i + window])

        if c == 0:
            for j in range(tiles):
                line = jnp.full((1, LANES), -1.0, jnp.float32)
                for h in range(per_tile):
                    k = j * per_tile + h
                    line = jnp.where(lane1 // cap == h, cells_r[k, t : t + 1, :], line)
                place[j * LANES : (j + 1) * LANES, :] = jnp.broadcast_to(line, (LANES, LANES)).T

        for j in range(tiles):
            part = recv[t, c, j * per_tile : (j + 1) * per_tile].reshape(LANES, width)
            hi, mid, lo = split3(part.T)
            spread[:, j * LANES : (j + 1) * LANES] = hi
            spread[:, slots + j * LANES : slots + (j + 1) * LANES] = mid
            spread[:, 2 * slots + j * LANES : 2 * slots + (j + 1) * LANES] = lo

        def add_forcing(y):
            col = lax.broadcasted_iota(jnp.int32, (slots, LANES), 1).astype(jnp.float32)
            where_to = place[...]
            hot = jnp.concatenate(
                [
                    jnp.where(where_to == col + float(v * LANES), 1.0, 0.0).astype(jnp.bfloat16)
                    for v in (y, y + 1)
                ],
                axis=1,
            )
            hot3 = jnp.concatenate([hot, hot, hot], axis=0)
            part = slice(base, base + width)
            got = jnp.dot(spread[...], hot3, preferred_element_type=jnp.float32)
            for v in (0, 1):
                new = got[:, v * LANES : (v + 1) * LANES]
                if not first:
                    new = new + state[t, y + v, part, :]
                state[t, y + v, part, :] = new * land[y + v]

        add_forcing(0)

        @pl.when(not_first)
        def _():
            halo_copy(t, c, False).start()

        add_forcing(rows - 2)

        @pl.when(not_last)
        def _():
            halo_copy(t, c, True).start()

        for y in range(2, rows - 2, 2):
            add_forcing(y)

        halves = chunk_blocks // 2

        @pl.loop(0, halves)
        def _(b):
            dst = pl.ds(pl.multiple_of(b * SUB, SUB), SUB)
            packed = jnp.zeros((SUB, LANES), jnp.float32)
            for half in (0, 1):
                for y in range(rows):
                    for f in range(fields):
                        q = half * (rows * fields) + y * fields + f
                        start = base + f * depth + (half * halves + b) * SUB
                        src = pl.ds(pl.multiple_of(start, SUB), SUB)
                        turned = pltpu.roll(state[t, y, src, :], (2 * q + 1) % LANES, 1)
                        packed = jnp.where(lane8 // 2 == q, turned, packed)
            side_s[t, c, dst, :] = packed

        for to_east in sides:
            side_copy(t, c, to_east).start()

        if c == chunks - 1:

            @pl.when(jnp.logical_not(is_ocean))
            def _():
                for f in range(fields):
                    for y in range(rows):
                        at = base + (f + 1) * depth - 1
                        top_s[t, f * rows + y : f * rows + y + 1, :] = state[t, y, at : at + 1, :]
                top_copy(t).start()

    def stepped_unit(i):
        t, c = units[i]
        base = c * width
        last = t == order[-1]
        nxt = order[min(order.index(t) + 1, steps - 1)]

        if i == 0:

            @pl.when(not_first)
            def _():
                north_rim_copy().wait_recv()

            east_rim_copy().wait_recv()

        for to_east in sides:
            side_copy(t, c, to_east).wait_recv()

        @pl.when(not_first)
        def _():
            halo_copy(t, c, True).wait_recv()

        @pl.when(not_last)
        def _():
            halo_copy(t, c, False).wait_recv()

        halves = chunk_blocks // 2

        @pl.loop(0, chunk_blocks)
        def _(b):
            half = b // halves
            level_block = c * chunk_blocks + b
            lev = pl.ds(pl.multiple_of(level_block * SUB, SUB), SUB)
            fls = [
                pl.ds(pl.multiple_of(base + f * depth + b * SUB, SUB), SUB) for f in range(fields)
            ]
            lo = pl.ds(pl.multiple_of(lax.rem(b, halves) * SUB, SUB), SUB)
            if lon_n == 2:
                edge = side_r[t, c, 1, lo, :]
            else:
                edge = jnp.where(
                    lax.rem(lane8, 2) == 1, side_r[t, c, 0, lo, :], side_r[t, c, 1, lo, :]
                )
            rim_e = rime_r[t]
            below = [halo[t, 0, s, :] for s in fls]
            here = [state[t, 0, s, :] for s in fls]
            fall_n = rimn_r[t, lev, :]
            for y in range(rows):
                if y < rows - 1:
                    above = [state[t, y + 1, s, :] for s in fls]
                else:
                    above = [halo[t, 1, s, :] for s in fls]
                line = pl.ds(level_block * (SUB * rows) + y, SUB, stride=rows)
                we, ke = vel_v[t, 0, line, :], dif_v[t, 0, line, :]
                wn, kn = vel_v[t, 1, line, :], dif_v[t, 1, line, :]
                up_e = jnp.maximum(we, 0.0) + ke
                fall_e = pltpu.roll(jnp.minimum(we, 0.0) - ke, 1, 1)
                q = level_block * rows + y
                from_west = pltpu.roll(rim_e, lax.rem(LANES - q, LANES), 1)
                fall_e = jnp.where(lane8 == 0, from_west, fall_e)
                up_n = jnp.maximum(wn, 0.0) + kn
                next_fall = jnp.minimum(wn, 0.0) - kn
                if y == rows - 1:
                    up_n = up_n * open_last
                for g in range(fields):
                    m = here[g]
                    q = half * (rows * fields) + y * fields + g
                    rim = pltpu.roll(edge, LANES - 1 - 2 * q, 1)
                    m_east = pltpu.roll(jnp.where(lane8 == 0, rim, m), LANES - 1, 1)
                    m_west = pltpu.roll(jnp.where(lane8 == LANES - 1, rim, m), 1, 1)
                    res = m
                    for f in range(fields):
                        res = res + mix_ref[f, g] * here[f]
                    res = res + up_e * (m_east - m) + fall_e * (m - m_west)
                    res = res + up_n * (above[g] - m) + fall_n * (m - below[g])
                    if last:
                        start = g * (levels * rows) + level_block * (SUB * rows) + y
                        out_ref[pl.ds(start, SUB, stride=rows), :] = res
                    else:
                        state[nxt, y, fls[g], :] = res
                below, here, fall_n = here, above, next_fall

    def couple(t):
        last = t == order[-1]
        nxt = order[min(order.index(t) + 1, steps - 1)]

        @pl.when(is_ocean)
        def _():
            top_copy(t).wait_recv()
            for g in range(fields):
                flux = air_ref[0, g] * top_r[t, 0:rows, :]
                for f in range(1, fields):
                    flux = flux + air_ref[f, g] * top_r[t, f * rows : (f + 1) * rows, :]
                flux = flux * sea_ref[...].astype(jnp.float32)
                if last:
                    spot = slice(g * levels * rows, g * levels * rows + rows)
                    out_ref[spot, :] = out_ref[spot, :] + flux
                else:
                    at = g * depth
                    for y in range(rows):
                        state[nxt, y, at : at + 1, :] = (
                            state[nxt, y, at : at + 1, :] + flux[y : y + 1, :]
                        )

    for i in range(len(units) + lag):
        if i < len(units):
            t, c = units[i]
            if c == 0 and i > 0:
                couple(order[order.index(t) - 1])
            forced_unit(i)
        if i >= lag:
            stepped_unit(i - lag)
    couple(order[-1])

    @pl.loop(1, n)
    def _(k):
        cell_copy(k).wait_send()
        for t, c in units:
            data_copy(t, c, k).wait_send()

    east_rim_copy().wait_send()

    @pl.when(not_last)
    def _():
        north_rim_copy().wait_send()

    for t, c in units:
        for to_east in sides:
            side_copy(t, c, to_east).wait_send()

        @pl.when(not_first)
        def _():
            halo_copy(t, c, False).wait_send()

        @pl.when(not_last)
        def _():
            halo_copy(t, c, True).wait_send()

    @pl.when(jnp.logical_not(is_ocean))
    def _():
        for t in order:
            top_copy(t).wait_send()


def shards(lat_n, lon_n, innovations, obs_owner, obs_cell, velocity, diffusion, mixing, air_sea, sea_mask):
    steps, levels, rows, cols = (velocity.shape[i] for i in (1, 3, 4, 5))
    fields = mixing.shape[1]
    obs = innovations.shape[2]
    fl = fields * levels
    n = lat_n * lon_n
    cap = max(SUB, 2 * obs // n)
    slots = n * cap
    tiles = slots // LANES
    chunks, lag, window = 2, 1, 2
    width = fl // chunks
    dims = (steps, fields, levels, rows, obs, lat_n, lon_n, cap, chunks, lag, window)
    vmem = pl.BlockSpec(memory_space=pltpu.VMEM)
    smem = pl.BlockSpec(memory_space=pltpu.SMEM)
    hbm = pl.BlockSpec(memory_space=pl.ANY)
    f32 = jnp.float32
    dma = pltpu.SemaphoreType.DMA
    out = pl.pallas_call(
        functools.partial(sweep, dims),
        out_shape=jax.ShapeDtypeStruct((fl * rows, cols), f32),
        in_specs=[hbm, vmem, vmem, hbm, hbm, smem, smem, vmem],
        out_specs=vmem,
        scratch_shapes=[
            pltpu.VMEM((steps, obs, fl), f32),
            pltpu.VMEM((steps, 2, levels * rows, cols), f32),
            pltpu.VMEM((steps, 2, levels * rows, cols), f32),
            pltpu.VMEM((steps, chunks, n, cap, width), f32),
            pltpu.VMEM((steps, chunks, n, cap, width), f32),
            pltpu.VMEM((tiles, SUB, LANES), f32),
            pltpu.VMEM((n, SUB, LANES), f32),
            pltpu.VMEM((steps, levels, cols), f32),
            pltpu.VMEM((steps, levels, cols), f32),
            pltpu.VMEM((steps, SUB, cols), f32),
            pltpu.VMEM((steps, SUB, cols), f32),
            pltpu.VMEM((steps, rows, fl, cols), f32),
            pltpu.VMEM((steps, 2, fl, cols), f32),
            pltpu.VMEM((steps, chunks, SUB * SUB // chunks, cols), f32),
            pltpu.VMEM((steps, chunks, 2, SUB * SUB // chunks, cols), f32),
            pltpu.VMEM((steps, fields * rows, cols), f32),
            pltpu.VMEM((steps, fields * rows, cols), f32),
            pltpu.VMEM((width, 3 * slots), jnp.bfloat16),
            pltpu.VMEM((slots, LANES), f32),
            dma((3, steps)),
            dma((steps * chunks, n)),
            dma((steps * chunks, n)),
            dma((n,)),
            dma((n,)),
            dma((2,)),
            dma((2,)),
            dma((steps * chunks, 2)),
            dma((steps * chunks, 2)),
            dma((steps * chunks, 2)),
            dma((steps * chunks, 2)),
            dma((steps,)),
            dma((steps,)),
        ],
        compiler_params=pltpu.CompilerParams(
            collective_id=0, has_side_effects=True, vmem_limit_bytes=56 * 1024 * 1024
        ),
    )(
        innovations[0],
        obs_owner.reshape(steps, 1, obs),
        obs_cell.reshape(steps, 1, obs),
        velocity[0].reshape(steps, 2, levels * rows, cols),
        diffusion[0].reshape(steps, 2, levels * rows, cols),
        mixing[0],
        air_sea,
        sea_mask,
    )
    return out.reshape(1, fields, levels, rows, cols)


def solution(mesh):
    return jax.shard_map(
        functools.partial(shards, mesh.shape["lat"], mesh.shape["lon"]),
        mesh=mesh,
        in_specs=(
            P("comp", None, ("lat", "lon"), None),
            P("comp", None, ("lat", "lon"), None),
            P("comp", None, ("lat", "lon")),
            P("comp", None, None, None, "lat", "lon"),
            P("comp", None, None, None, "lat", "lon"),
            P("comp", None, None),
            P(),
            P("lat", "lon"),
        ),
        out_specs=P("comp", None, None, "lat", "lon"),
        check_vma=False,
    )
```

```python
import functools

import jax
import jax.numpy as jnp
from jax import lax
from jax.experimental import pallas as pl
from jax.experimental.pallas import tpu as pltpu
from jax.sharding import PartitionSpec as P

MESH = pl.DeviceIdType.MESH
LANES = 128
SUB = 8


def split2(x):
    hi = x.astype(jnp.bfloat16)
    return hi, (x - hi.astype(jnp.float32)).astype(jnp.bfloat16)


def sweep(
    dims,
    innov,
    owner_ref,
    cell_ref,
    vel,
    dif,
    mix_ref,
    air_ref,
    sea_ref,
    out_ref,
    inn_v,
    vel_v,
    dif_v,
    send,
    recv,
    cells_s,
    cells_r,
    rimn_s,
    rimn_r,
    rime_s,
    rime_r,
    state,
    halo,
    side_s,
    side_r,
    top_s,
    top_r,
    spread,
    place,
    picked,
    coef,
    load_sem,
    data_ss,
    data_rs,
    cell_ss,
    cell_rs,
    rim_ss,
    rim_rs,
    halo_ss,
    halo_rs,
    side_ss,
    side_rs,
    top_ss,
    top_rs,
):
    steps, fields, levels, rows, obs, lat_n, lon_n, cap, chunks, lag, window = dims
    n = lat_n * lon_n
    slots = n * cap
    tiles = slots // LANES
    per_tile = LANES // cap
    fl = fields * levels
    blocks = levels // SUB
    depth = levels // chunks
    width = fields * depth
    chunk_blocks = depth // SUB
    comp = lax.axis_index("comp")
    lat = lax.axis_index("lat")
    lon = lax.axis_index("lon")
    me = lat * lon_n + lon
    east = lax.rem(lon + 1, lon_n)
    west = lax.rem(lon + lon_n - 1, lon_n)
    is_ocean = comp == 1
    order = list(reversed(range(steps)))
    units = [(t, c) for t in order for c in range(chunks)]

    def at_offset(k):
        peer = lax.rem(me + k, n)
        return (comp, lax.div(peer, lon_n), lax.rem(peer, lon_n))

    loads = {}
    for t in order:
        loads["i", t] = pltpu.make_async_copy(innov.at[t], inn_v.at[t], load_sem.at[0, t])
        loads["i", t].start()
    for t in order:
        loads["v", t] = pltpu.make_async_copy(vel.at[t], vel_v.at[t], load_sem.at[1, t])
        loads["d", t] = pltpu.make_async_copy(dif.at[t], dif_v.at[t], load_sem.at[2, t])
        loads["v", t].start()
        loads["d", t].start()

    barrier = pltpu.get_barrier_semaphore()

    @pl.loop(1, n)
    def _(k):
        pl.semaphore_signal(barrier, inc=1, device_id=at_offset(k), device_id_type=MESH)

    pl.semaphore_signal(barrier, inc=1, device_id=(1 - comp, lat, lon), device_id_type=MESH)

    sub_i = lax.broadcasted_iota(jnp.int32, (obs, obs), 0)
    lane_i = lax.broadcasted_iota(jnp.int32, (obs, obs), 1)
    earlier = sub_i < lane_i
    lane1 = lax.broadcasted_iota(jnp.int32, (1, LANES), 1)
    lane8 = lax.broadcasted_iota(jnp.int32, (SUB, LANES), 1)

    def picks(t):
        owner = owner_ref[t]
        across = jnp.broadcast_to(owner.astype(jnp.float32), (obs, obs))
        down = across.T
        rank = jnp.sum(
            jnp.where((across == down) & earlier, 1.0, 0.0), axis=0, keepdims=True
        ).astype(jnp.int32)
        shift = owner - me
        offset = jnp.where(shift < 0, shift + n, shift)
        target = offset * cap + rank
        slot_i = lax.broadcasted_iota(jnp.int32, (slots, obs), 0)
        return jnp.where(slot_i == target, 1.0, 0.0)

    def columns(t):
        number = jnp.broadcast_to(cell_ref[t] + 1, (2 * SUB, obs))
        row16 = lax.broadcasted_iota(jnp.int32, (2 * SUB, obs), 0)
        coarse = lax.shift_right_logical(number, 5)
        parts = jnp.where(row16 == 0, coarse * 32, jnp.where(row16 == 1, number - coarse * 32, 0))
        at = lax.dot_general(
            parts.astype(jnp.float32).astype(jnp.bfloat16),
            picked[t],
            (((1,), (1,)), ((), ())),
            preferred_element_type=jnp.float32,
        )
        at = at[0:1, :] + at[1:2, :] - 1.0
        for i in range(tiles):
            cells_s[i, t : t + 1, :] = at[0:1, i * LANES : (i + 1) * LANES]

    pl.semaphore_wait(barrier, n)

    def cell_copy(k):
        return pltpu.make_async_remote_copy(
            src_ref=cells_s.at[k // per_tile],
            dst_ref=cells_r.at[k],
            send_sem=cell_ss.at[0],
            recv_sem=cell_rs.at[0],
            device_id=at_offset(k),
            device_id_type=MESH,
        )

    def data_copy(t, c, k):
        return pltpu.make_async_remote_copy(
            src_ref=send.at[t, c, k],
            dst_ref=recv.at[t, c, k],
            send_sem=data_ss.at[t * chunks + c],
            recv_sem=data_rs.at[t * chunks + c],
            device_id=at_offset(k),
            device_id_type=MESH,
        )

    def data_all(t, c):
        return pltpu.make_async_remote_copy(
            src_ref=send.at[t, c, pl.ds(1, n - 1)],
            dst_ref=recv.at[t, c, pl.ds(1, n - 1)],
            send_sem=data_ss.at[t * chunks + c],
            recv_sem=data_rs.at[t * chunks + c],
            device_id=at_offset(1),
            device_id_type=MESH,
        )

    def cells_all():
        part = cells_r.at[pl.ds(1, n - 1)]
        return pltpu.make_async_remote_copy(
            src_ref=part,
            dst_ref=part,
            send_sem=cell_ss.at[0],
            recv_sem=cell_rs.at[0],
            device_id=at_offset(1),
            device_id_type=MESH,
        )

    def north_rim_copy():
        return pltpu.make_async_remote_copy(
            src_ref=rimn_s,
            dst_ref=rimn_r,
            send_sem=rim_ss.at[0],
            recv_sem=rim_rs.at[0],
            device_id=(comp, lax.rem(lat + 1, lat_n), lon),
            device_id_type=MESH,
        )

    def east_rim_copy():
        return pltpu.make_async_remote_copy(
            src_ref=rime_s,
            dst_ref=rime_r,
            send_sem=rim_ss.at[1],
            recv_sem=rim_rs.at[1],
            device_id=(comp, lat, east),
            device_id_type=MESH,
        )

    def halo_copy(t, c, up):
        part = pl.ds(c * width, width)
        return pltpu.make_async_remote_copy(
            src_ref=state.at[t, rows - 1 if up else 0, part],
            dst_ref=halo.at[t, 0 if up else 1, part],
            send_sem=halo_ss.at[t * chunks + c, 0 if up else 1],
            recv_sem=halo_rs.at[t * chunks + c, 0 if up else 1],
            device_id=(comp, lax.rem(lat + (1 if up else lat_n - 1), lat_n), lon),
            device_id_type=MESH,
        )

    def side_copy(t, c, to_east):
        return pltpu.make_async_remote_copy(
            src_ref=side_s.at[t, c],
            dst_ref=side_r.at[t, c, 1 if to_east else 0],
            send_sem=side_ss.at[t * chunks + c, 1 if to_east else 0],
            recv_sem=side_rs.at[t * chunks + c, 1 if to_east else 0],
            device_id=(comp, lat, east if to_east else west),
            device_id_type=MESH,
        )

    def top_copy(t):
        return pltpu.make_async_remote_copy(
            src_ref=top_s.at[t],
            dst_ref=top_r.at[t],
            send_sem=top_ss.at[t],
            recv_sem=top_rs.at[t],
            device_id=(1 - comp, lat, lon),
            device_id_type=MESH,
        )

    sides = (True,) if lon_n == 2 else (True, False)
    not_last = lat < lat_n - 1
    not_first = lat > 0

    def pack(t):
        loads["i", t].wait()
        hot = picks(t).astype(jnp.bfloat16)
        picked[t] = hot
        wide = inn_v[t]
        by_chunk = jnp.concatenate(
            [
                wide[:, f * levels + c * depth : f * levels + (c + 1) * depth]
                for c in range(chunks)
                for f in range(fields)
            ],
            axis=1,
        )
        packed = jnp.dot(
            jnp.concatenate([hot, hot], axis=1),
            jnp.concatenate(split2(by_chunk), axis=0),
            preferred_element_type=jnp.float32,
        )
        for c in range(chunks):
            part = packed[:, c * width : (c + 1) * width].reshape(n, cap, width)
            send[t, c] = part
            recv[t, c, 0] = part[0]

    def ship(t, c):
        @pl.loop(1, n)
        def _(k):
            data_copy(t, c, k).start()

    pack(order[0])
    for i in range(min(window, chunks)):
        ship(*units[i])
    for t in order[1:]:
        pack(t)
    for t in order:
        columns(t)

    @pl.loop(1, n)
    def _(k):
        cell_copy(k).start()

    cells_r[0] = cells_s[0]
    for i in range(chunks, min(window, len(units))):
        ship(*units[i])

    for t in order:
        loads["v", t].wait()
        loads["d", t].wait()

        @pl.loop(0, blocks)
        def _(b):
            packed = rime_s[t]
            lev = pl.ds(pl.multiple_of(b * SUB, SUB), SUB)
            for y in range(rows):
                line = pl.ds(b * (SUB * rows) + y, SUB, stride=rows)
                we, ke = vel_v[t, 0, line, :], dif_v[t, 0, line, :]
                wn, kn = vel_v[t, 1, line, :], dif_v[t, 1, line, :]
                fall_e = jnp.minimum(we, 0.0) - ke
                q = b * rows + y
                packed = jnp.where(
                    lane8 == q, pltpu.roll(fall_e, lax.rem(q + 1, LANES), 1), packed
                )
                up_n = jnp.maximum(wn, 0.0) + kn
                fall_n = jnp.minimum(wn, 0.0) - kn
                if y == rows - 1:
                    up_n = up_n * jnp.where(not_last, 1.0, 0.0)
                    rimn_s[t, lev, :] = fall_n
                coef[t, 0, y, lev, :] = jnp.maximum(we, 0.0) + ke
                coef[t, 1, y, lev, :] = pltpu.roll(fall_e, 1, 1)
                coef[t, 2, y, lev, :] = up_n
                coef[t, 3, y, lev, :] = fall_n
            rime_s[t] = packed

    @pl.when(not_last)
    def _():
        north_rim_copy().start()

    east_rim_copy().start()

    @pl.when(jnp.logical_not(not_first))
    def _():
        rimn_r[...] = jnp.zeros_like(rimn_r)
        for t in order:
            halo[t, 0] = jnp.zeros((fl, LANES), jnp.float32)

    @pl.when(jnp.logical_not(not_last))
    def _():
        for t in order:
            halo[t, 1] = jnp.zeros((fl, LANES), jnp.float32)

    cells_all().wait_recv()

    land = [
        jnp.where(is_ocean, sea_ref[y : y + 1, :].astype(jnp.float32), 1.0) for y in range(rows)
    ]

    def forced_unit(i):
        t, c = units[i]
        first = t == order[0]
        base = c * width

        data_all(t, c).wait_recv()

        if i + window < len(units):
            ship(*units[i + window])

        if c == 0:
            for j in range(tiles):
                line = jnp.full((1, LANES), -1.0, jnp.float32)
                for h in range(per_tile):
                    k = j * per_tile + h
                    line = jnp.where(lane1 // cap == h, cells_r[k, t : t + 1, :], line)
                place[j * LANES : (j + 1) * LANES, :] = jnp.broadcast_to(line, (LANES, LANES)).T

        for j in range(tiles):
            part = recv[t, c, j * per_tile : (j + 1) * per_tile].reshape(LANES, width)
            hi, rest = split2(part.T)
            spread[:, j * LANES : (j + 1) * LANES] = hi
            spread[:, slots + j * LANES : slots + (j + 1) * LANES] = rest

        def add_forcing(y):
            col = lax.broadcasted_iota(jnp.int32, (slots, LANES), 1).astype(jnp.float32)
            where_to = place[...]
            hot = jnp.concatenate(
                [
                    jnp.where(where_to == col + float(v * LANES), 1.0, 0.0).astype(jnp.bfloat16)
                    for v in (y, y + 1)
                ],
                axis=1,
            )
            hot2 = jnp.concatenate([hot, hot], axis=0)
            part = slice(base, base + width)
            got = jnp.dot(spread[...], hot2, preferred_element_type=jnp.float32)
            for v in (0, 1):
                new = got[:, v * LANES : (v + 1) * LANES]
                if not first:
                    new = new + state[t, y + v, part, :]
                state[t, y + v, part, :] = new * land[y + v]

        add_forcing(0)

        @pl.when(not_first)
        def _():
            halo_copy(t, c, False).start()

        add_forcing(rows - 2)

        @pl.when(not_last)
        def _():
            halo_copy(t, c, True).start()

        for y in range(2, rows - 2, 2):
            add_forcing(y)

        halves = chunk_blocks // 2

        @pl.loop(0, halves)
        def _(b):
            dst = pl.ds(pl.multiple_of(b * SUB, SUB), SUB)
            packed = jnp.zeros((SUB, LANES), jnp.float32)
            for half in (0, 1):
                for y in range(rows):
                    for f in range(fields):
                        q = half * (rows * fields) + y * fields + f
                        start = base + f * depth + (half * halves + b) * SUB
                        src = pl.ds(pl.multiple_of(start, SUB), SUB)
                        turned = pltpu.roll(state[t, y, src, :], (2 * q + 1) % LANES, 1)
                        packed = jnp.where(lane8 // 2 == q, turned, packed)
            side_s[t, c, dst, :] = packed

        for to_east in sides:
            side_copy(t, c, to_east).start()

        if c == chunks - 1:

            @pl.when(jnp.logical_not(is_ocean))
            def _():
                for f in range(fields):
                    for y in range(rows):
                        at = base + (f + 1) * depth - 1
                        top_s[t, f * rows + y : f * rows + y + 1, :] = state[t, y, at : at + 1, :]
                top_copy(t).start()

    def stepped_unit(i):
        t, c = units[i]
        base = c * width
        last = t == order[-1]
        nxt = order[min(order.index(t) + 1, steps - 1)]

        if i == 0:

            @pl.when(not_first)
            def _():
                north_rim_copy().wait_recv()

            east_rim_copy().wait_recv()

        for to_east in sides:
            side_copy(t, c, to_east).wait_recv()

        @pl.when(not_first)
        def _():
            halo_copy(t, c, True).wait_recv()

        @pl.when(not_last)
        def _():
            halo_copy(t, c, False).wait_recv()

        halves = chunk_blocks // 2

        @pl.loop(0, chunk_blocks, unroll=2)
        def _(b):
            half = b // halves
            level_block = c * chunk_blocks + b
            lev = pl.ds(pl.multiple_of(level_block * SUB, SUB), SUB)
            fls = [
                pl.ds(pl.multiple_of(base + f * depth + b * SUB, SUB), SUB) for f in range(fields)
            ]
            lo = pl.ds(pl.multiple_of(lax.rem(b, halves) * SUB, SUB), SUB)
            if lon_n == 2:
                edge = side_r[t, c, 1, lo, :]
            else:
                edge = jnp.where(
                    lax.rem(lane8, 2) == 1, side_r[t, c, 0, lo, :], side_r[t, c, 1, lo, :]
                )
            even = lax.rem(lane8, 2) == 0
            edge = jnp.where(even, pltpu.roll(edge, LANES - 1, 1), pltpu.roll(edge, 1, 1))
            rim_e = rime_r[t]
            below = [halo[t, 0, s, :] for s in fls]
            here = [state[t, 0, s, :] for s in fls]
            fall_n = rimn_r[t, lev, :]
            for y in range(rows):
                if y < rows - 1:
                    above = [state[t, y + 1, s, :] for s in fls]
                else:
                    above = [halo[t, 1, s, :] for s in fls]
                q = level_block * rows + y
                from_west = pltpu.roll(rim_e, lax.rem(LANES - q, LANES), 1)
                up_e = coef[t, 0, y, lev, :]
                fall_e = jnp.where(lane8 == 0, from_west, coef[t, 1, y, lev, :])
                up_n = coef[t, 2, y, lev, :]
                next_fall = coef[t, 3, y, lev, :]
                for g in range(fields):
                    m = here[g]
                    q = half * (rows * fields) + y * fields + g
                    rim = pltpu.roll(edge, LANES - 1 - 2 * q, 1)
                    m_east = jnp.where(lane8 == LANES - 1, rim, pltpu.roll(m, LANES - 1, 1))
                    m_west = jnp.where(lane8 == 0, rim, pltpu.roll(m, 1, 1))
                    res = m
                    for f in range(fields):
                        res = res + mix_ref[f, g] * here[f]
                    res = res + up_e * (m_east - m) + fall_e * (m - m_west)
                    res = res + up_n * (above[g] - m) + fall_n * (m - below[g])
                    if last:
                        start = g * (levels * rows) + level_block * (SUB * rows) + y
                        out_ref[pl.ds(start, SUB, stride=rows), :] = res
                    else:
                        state[nxt, y, fls[g], :] = res
                below, here, fall_n = here, above, next_fall

    def couple(t):
        last = t == order[-1]
        nxt = order[min(order.index(t) + 1, steps - 1)]

        @pl.when(is_ocean)
        def _():
            top_copy(t).wait_recv()
            for g in range(fields):
                flux = air_ref[0, g] * top_r[t, 0:rows, :]
                for f in range(1, fields):
                    flux = flux + air_ref[f, g] * top_r[t, f * rows : (f + 1) * rows, :]
                flux = flux * sea_ref[...].astype(jnp.float32)
                if last:
                    spot = slice(g * levels * rows, g * levels * rows + rows)
                    out_ref[spot, :] = out_ref[spot, :] + flux
                else:
                    at = g * depth
                    for y in range(rows):
                        state[nxt, y, at : at + 1, :] = (
                            state[nxt, y, at : at + 1, :] + flux[y : y + 1, :]
                        )

    for i in range(len(units) + lag):
        if i < len(units):
            t, c = units[i]
            if c == 0 and i > 0:
                couple(order[order.index(t) - 1])
            forced_unit(i)
        if i >= lag:
            stepped_unit(i - lag)
    couple(order[-1])

    cells_all().wait_send()
    for t, c in units:
        data_all(t, c).wait_send()

    east_rim_copy().wait_send()

    @pl.when(not_last)
    def _():
        north_rim_copy().wait_send()

    for t, c in units:
        for to_east in sides:
            side_copy(t, c, to_east).wait_send()

        @pl.when(not_first)
        def _():
            halo_copy(t, c, False).wait_send()

        @pl.when(not_last)
        def _():
            halo_copy(t, c, True).wait_send()

    @pl.when(jnp.logical_not(is_ocean))
    def _():
        for t in order:
            top_copy(t).wait_send()


def shards(lat_n, lon_n, innovations, obs_owner, obs_cell, velocity, diffusion, mixing, air_sea, sea_mask):
    steps, levels, rows, cols = (velocity.shape[i] for i in (1, 3, 4, 5))
    fields = mixing.shape[1]
    obs = innovations.shape[2]
    fl = fields * levels
    n = lat_n * lon_n
    cap = max(SUB, 2 * obs // n)
    slots = n * cap
    tiles = slots // LANES
    chunks, lag, window = 2, 1, 2
    width = fl // chunks
    dims = (steps, fields, levels, rows, obs, lat_n, lon_n, cap, chunks, lag, window)
    vmem = pl.BlockSpec(memory_space=pltpu.VMEM)
    smem = pl.BlockSpec(memory_space=pltpu.SMEM)
    hbm = pl.BlockSpec(memory_space=pl.ANY)
    f32 = jnp.float32
    dma = pltpu.SemaphoreType.DMA
    out = pl.pallas_call(
        functools.partial(sweep, dims),
        out_shape=jax.ShapeDtypeStruct((fl * rows, cols), f32),
        in_specs=[hbm, vmem, vmem, hbm, hbm, smem, smem, vmem],
        out_specs=vmem,
        scratch_shapes=[
            pltpu.VMEM((steps, obs, fl), f32),
            pltpu.VMEM((steps, 2, levels * rows, cols), f32),
            pltpu.VMEM((steps, 2, levels * rows, cols), f32),
            pltpu.VMEM((steps, chunks, n, cap, width), f32),
            pltpu.VMEM((steps, chunks, n, cap, width), f32),
            pltpu.VMEM((tiles, SUB, LANES), f32),
            pltpu.VMEM((n, SUB, LANES), f32),
            pltpu.VMEM((steps, levels, cols), f32),
            pltpu.VMEM((steps, levels, cols), f32),
            pltpu.VMEM((steps, SUB, cols), f32),
            pltpu.VMEM((steps, SUB, cols), f32),
            pltpu.VMEM((steps, rows, fl, cols), f32),
            pltpu.VMEM((steps, 2, fl, cols), f32),
            pltpu.VMEM((steps, chunks, SUB * SUB // chunks, cols), f32),
            pltpu.VMEM((steps, chunks, 2, SUB * SUB // chunks, cols), f32),
            pltpu.VMEM((steps, fields * rows, cols), f32),
            pltpu.VMEM((steps, fields * rows, cols), f32),
            pltpu.VMEM((width, 2 * slots), jnp.bfloat16),
            pltpu.VMEM((slots, LANES), f32),
            pltpu.VMEM((steps, slots, obs), jnp.bfloat16),
            pltpu.VMEM((steps, 4, rows, levels, cols), f32),
            dma((3, steps)),
            dma((steps * chunks,)),
            dma((steps * chunks,)),
            dma((1,)),
            dma((1,)),
            dma((2,)),
            dma((2,)),
            dma((steps * chunks, 2)),
            dma((steps * chunks, 2)),
            dma((steps * chunks, 2)),
            dma((steps * chunks, 2)),
            dma((steps,)),
            dma((steps,)),
        ],
        compiler_params=pltpu.CompilerParams(
            collective_id=0, has_side_effects=True, vmem_limit_bytes=56 * 1024 * 1024
        ),
    )(
        innovations[0],
        obs_owner.reshape(steps, 1, obs),
        obs_cell.reshape(steps, 1, obs),
        velocity[0].reshape(steps, 2, levels * rows, cols),
        diffusion[0].reshape(steps, 2, levels * rows, cols),
        mixing[0],
        air_sea,
        sea_mask,
    )
    return out.reshape(1, fields, levels, rows, cols)


def solution(mesh):
    return jax.shard_map(
        functools.partial(shards, mesh.shape["lat"], mesh.shape["lon"]),
        mesh=mesh,
        in_specs=(
            P("comp", None, ("lat", "lon"), None),
            P("comp", None, ("lat", "lon"), None),
            P("comp", None, ("lat", "lon")),
            P("comp", None, None, None, "lat", "lon"),
            P("comp", None, None, None, "lat", "lon"),
            P("comp", None, None),
            P(),
            P("lat", "lon"),
        ),
        out_specs=P("comp", None, None, "lat", "lon"),
        check_vma=False,
    )
```
